32 devices in a mesh: blk: 8 (over z, y), sub: 4 (over x, core).
Axes of the slice: x: 2, y: 2, z: 4, core: 2. Of those that a mesh axis runs over, the one named last changes fastest.
Arguments:
- fields: float32 [8, 4, 16, 64, 1024], P('blk', None, None, 'sub'), may hold values from 0.05 to 3, as said below
- block_speed: float32 [8], P('blk'), may hold values from 0.5 to 2
- neighbours: int32 [8, 2], replicated, may hold values from 0 to 7, as said below
- block_slot: int32 [8], replicated, may hold values from 0 to 7, each once
- table_base: int32 [8, 2, 16], replicated, may hold values from 0 to 15
- table_weight: float32 [8, 2, 16], replicated, may hold values from 0 to 1
- start_basis: float32 [512, 32], replicated, may hold values from -6 to 6
Outputs:
- section_fields: float32 [8, 4, 16, 64, 1024], P('blk', None, None, 'sub')
- interface_penalty: float32 [8, 2, 4, 16, 64], P('blk', None, None, None, 'sub')
- mode_basis: float32 [512, 32], replicated
- tucker_core: float32 [32, 8192], P(None, ('blk', 'sub'))
The draws below stay inside these ranges and needn't reach their ends.
Inputs may be any that keep to these rules, and one draw needn't show every extreme that they name: fields[:, 0] (temperature) lies in [1, 3] and fields[:, 1:] (mass fractions) in [0.05, 1]. neighbours[b, 0] is the block whose high face meets block b's low face and neighbours[b, 1] the block whose low face meets its high face; neighbours[neighbours[b, 1], 0] = b, and following the second entry visits every block once. `block_slot`: each slot holds exactly one block.
All inputs are finite; a program needn't handle non-finite values.
Results may differ from the reference program's by a relative error of at most 0.003.
Values sent between devices are 32-bit elements; how exact they have to be, the bound alone decides.
A program may use at most 128 MiB of HBM per device.

```python
import math
import jax
import jax.numpy as jnp
from jax import lax

NVAR = 4
MODE = 512
RANK = 32
ITERS = 4
BX = 16
CY = 16
BZ = 1024
NBLOCKS = 8
BY = 64
COLS = 8192
N_SUB = 4


def draw_fields(key, part):
    uniform_part = jax.random.uniform(key, (NBLOCKS, NVAR, BX, BY, BZ), jnp.float32)
    lowest = jnp.array([1.0, 0.05, 0.05, 0.05], jnp.float32).reshape(4, 1, 1, 1)
    ranges = jnp.array([2.0, 0.95, 0.95, 0.95], jnp.float32).reshape(4, 1, 1, 1)
    return lowest + ranges * uniform_part


def draw_neighbours(key, part):
    chain_order = jax.random.permutation(key, NBLOCKS).astype(jnp.int32)
    following = jnp.roll(chain_order, -1)
    preceding = jnp.roll(chain_order, 1)
    neighbour_pairs = jnp.stack([preceding, following], axis=1)
    return jnp.zeros((NBLOCKS, 2), jnp.int32).at[chain_order].set(neighbour_pairs)


def touch_ends(values, key, low, largest):
    longest = values.shape.index(max(values.shape))
    spots = []
    for shift in (0, 1):
        where = [jax.random.randint(jax.random.fold_in(key, axis), (), 0, length) for axis, length in enumerate(values.shape)]
        where[longest] = (where[longest] + shift) % values.shape[longest]
        spots.append(tuple(where))
    return values.at[spots[0]].set(low).at[spots[1]].set(largest)


def block_scale(key, dims, cuts, least, high):
    def one(axis_at, shards_of):
        steps = jax.random.uniform(jax.random.fold_in(jax.random.fold_in(key, 6), axis_at), (shards_of,), jnp.float32, least / len(cuts), high / len(cuts))
        return jnp.repeat(jnp.exp(steps), dims[axis_at] // shards_of).reshape((-1,) + (1,) * (len(dims) - axis_at - 1))

    level = one(*cuts[0])
    for cut in cuts[1:]:
        level = level * one(*cut)
    return level


def noise(rng, extent, scale, limit, kind=jnp.bfloat16):
    drawn = jax.random.normal(rng, extent, jnp.float32) * scale
    return jnp.minimum(jnp.maximum(drawn, -limit), limit).astype(kind)


def setup_inputs(seed: int = 0) -> dict:
    key_list = jax.random.split(jax.random.key(seed), 8)
    return {
        "fields": draw_fields(jax.random.fold_in(key_list[7], 71), 0),
        "block_speed": jnp.clip(jnp.exp(math.log(2.0) - 1.3862944 * jax.random.uniform(key_list[1], (NBLOCKS,), jnp.float32) ** block_scale(key_list[1], (NBLOCKS,), ((0, 8),), -0.2, 0.2)), 0.5, 2.0),
        "neighbours": draw_neighbours(jax.random.fold_in(key_list[7], 71), 0),
        "block_slot": jax.random.permutation(key_list[3], NBLOCKS).astype(jnp.int32),
        "table_base": touch_ends(jax.random.randint(key_list[4], (NBLOCKS, 2, BX), 0, BX), jax.random.fold_in(key_list[4], 1), 0, BX - 1).astype(jnp.int32),
        "table_weight": jnp.clip(jax.random.uniform(key_list[5], (NBLOCKS, 2, BX), jnp.float32, 0.0, 1.0), 0.0, 1.0),
        "start_basis": noise(key_list[6], (MODE, RANK), 1.0, 6.0, jnp.float32),
    }


time_step = 0.1
diffusivity = 0.5
prefactor = 5.0
activation = 4.0
heat_release = 2.0
oxidizer_ratio = 1.5

def levels():
    return jnp.array([2.0, 0.525, 0.525, 0.525], jnp.float32).reshape(4, 1, 1, 1)

def streamwise(values):
    ahead = values[..., 2:]
    behind = values[..., :-2]
    slope = jnp.concatenate([values[..., 1:2] - values[..., 0:1], (ahead - behind) * 0.5, values[..., -1:] - values[..., -2:-1]], axis=-1)
    curve = jnp.concatenate([values[..., 0:1] - 2.0 * values[..., 1:2] + values[..., 2:3], ahead - 2.0 * values[..., 1:-1] + behind, values[..., -1:] - 2.0 * values[..., -2:-1] + values[..., -3:-2]], axis=-1)
    return (slope, curve)

def section_rate(values, span_ahead, span_behind, speed_value, inflow, outflow):
    along_x = jnp.roll(values, -1, 1) + jnp.roll(values, 1, 1) - 2.0 * values
    along_y = span_ahead + span_behind - 2.0 * values
    slope, curve = streamwise(values)
    rate = prefactor * values[1] * values[2] * jnp.exp(-activation / values[0])
    source = jnp.stack([heat_release * rate, -rate, -oxidizer_ratio * rate, (1.0 + oxidizer_ratio) * rate])
    rhs = -speed_value * slope + diffusivity * (along_x + along_y + curve) + source
    low_penalty = -2.0 * (speed_value + diffusivity) * (values[..., 0] - inflow)
    high_penalty = -2.0 * diffusivity * (values[..., -1] - outflow)
    rhs = rhs.at[..., 0].add(low_penalty)
    rhs = rhs.at[..., -1].add(high_penalty)
    return (values + time_step * rhs, jnp.stack([low_penalty, high_penalty]))

def interpolate(face, base_nodes, fractions):
    width_x = face.shape[2]
    first_index = jnp.broadcast_to(base_nodes[:, None, :, None], face.shape)
    second_index = jnp.broadcast_to(((base_nodes + 1) % width_x)[:, None, :, None], face.shape)
    first = jnp.take_along_axis(face, first_index, axis=2)
    second = jnp.take_along_axis(face, second_index, axis=2)
    return (1.0 - fractions)[:, None, :, None] * first + fractions[:, None, :, None] * second

def orthonormal(columns):
    inner = jnp.dot(columns.T, columns, precision=lax.Precision.HIGHEST)
    factor = jnp.linalg.cholesky(inner)
    return lax.linalg.triangular_solve(factor, columns, left_side=False, lower=True, transpose_a=True)

def reference(fields, block_speed, neighbours, block_slot, table_base, table_weight, start_basis):
    block_ids = jnp.arange(NBLOCKS, dtype=jnp.int32)
    block_of = lax.optimization_barrier(jnp.sum(jnp.where(block_slot[:, None] == block_ids[None, :], block_ids[:, None], 0), axis=0)).astype(jnp.int32)
    low_slots = block_slot[neighbours[block_of, 0]]
    high_slots = block_slot[neighbours[block_of, 1]]
    high_faces = fields[low_slots, :, :, :, BZ - 1]
    low_faces = fields[high_slots, :, :, :, 0]
    bases = table_base[block_of]
    weights = table_weight[block_of]
    inflow_all = interpolate(high_faces, bases[:, 0], weights[:, 0])
    outflow_all = interpolate(low_faces, bases[:, 1], weights[:, 1])

    def one_slot(items):
        values, speed_value, inflow, outflow = items
        return section_rate(values, jnp.roll(values, -1, 2), jnp.roll(values, 1, 2), speed_value, inflow, outflow)
    section_fields, interface_penalty = lax.map(one_slot, (fields, block_speed, inflow_all, outflow_all))
    coarse = (fields[:, :, ::2, ::2, ::2] - levels()[None]).astype(jnp.bfloat16)
    coarse = coarse.reshape(NBLOCKS, NVAR, BX // 2, N_SUB, CY // 2, MODE)
    matrix = jnp.transpose(coarse, (0, 3, 1, 2, 4, 5)).reshape(COLS, MODE)
    matrix = lax.optimization_barrier(matrix)
    gram = jnp.dot(matrix.T.astype(jnp.float32), matrix.astype(jnp.float32), preferred_element_type=jnp.float32) / COLS
    basis = start_basis
    for iteration in range(ITERS):
        basis = orthonormal(jnp.dot(gram, basis, precision=lax.Precision.HIGHEST))
    widened = matrix.astype(jnp.float32)
    core = jnp.dot(basis.T, widened.T, precision=lax.Precision.HIGHEST) / math.sqrt(MODE)
    return (section_fields, interface_penalty, basis, core)
```

```python
import functools
import math

import jax
import jax.numpy as jnp
from jax import lax
from jax.experimental import pallas as pl
from jax.experimental.pallas import tpu as pltpu
from jax.sharding import PartitionSpec as P

ITERS = 4
LEVELS = (2.0, 0.525, 0.525, 0.525)
PIECES = 32
GROUP = 4
TIME_STEP = 0.1
DIFFUSIVITY = 0.5
PREFACTOR = 5.0
ACTIVATION = 4.0
HEAT_RELEASE = 2.0
OXIDIZER_RATIO = 1.5
F32 = jnp.float32
BF16 = jnp.bfloat16
MESH = pl.DeviceIdType.MESH
NT = (((1,), (1,)), ((), ()))
NN = (((1,), (0,)), ((), ()))


def dot(a, b, dims, precision=None):
    return lax.dot_general(a, b, dims, precision=precision, preferred_element_type=F32)


def split3(a):
    high = a.astype(BF16)
    rest = a - high.astype(F32)
    mid = rest.astype(BF16)
    low = (rest - mid.astype(F32)).astype(BF16)
    return jnp.concatenate([high, mid, low], axis=0)


def join3(a):
    n = a.shape[0] // 3
    return (a[2 * n :] + a[n : 2 * n]) + a[:n]


def factor_apply(wt):
    rank, mode = wt.shape
    zeros = jnp.zeros((rank, mode), F32)
    inner = dot(
        wt, jnp.concatenate([wt, zeros, zeros, zeros], axis=0), NT, lax.Precision.HIGHEST
    )
    row = lax.broadcasted_iota(jnp.int32, (rank, 128), 0)
    lane = lax.broadcasted_iota(jnp.int32, (rank, 128), 1)
    inner = inner + jnp.where(lane == row + rank, 1.0, 0.0)
    blocks = [inner[8 * i : 8 * i + 8] for i in range(rank // 8)]
    sub8 = lax.broadcasted_iota(jnp.int32, (8, 128), 0)
    full = (8, 128)
    done = [jnp.zeros(full, F32) for _ in blocks]
    for k in range(0, rank, GROUP):
        kb, kr = k // 8, k % 8
        rows = [
            jnp.broadcast_to(blocks[kb][kr + l : kr + l + 1], full) for l in range(GROUP)
        ]
        elem = [
            [
                jnp.broadcast_to(rows[l][:, k + j : k + j + 1], full) if j >= l else None
                for j in range(GROUP)
            ]
            for l in range(GROUP)
        ]
        rest = [b for b in range(kb, len(blocks)) if b > kb or kr + GROUP < 8]
        cols = {
            b: [jnp.broadcast_to(blocks[b][:, k + j : k + j + 1], full) for j in range(GROUP)]
            for b in rest
        }
        for j in range(GROUP):
            scale = 1.0 / elem[j][j]
            root = lax.rsqrt(elem[j][j])
            done[kb] = jnp.where(sub8 == kr + j, rows[j] * root, done[kb])
            ratio = [
                elem[j][l] * scale if l > j else None for l in range(GROUP)
            ]
            for l in range(j + 1, GROUP):
                rows[l] = rows[l] - ratio[l] * rows[j]
                for m in range(l, GROUP):
                    elem[l][m] = elem[l][m] - ratio[l] * elem[j][m]
            for b in rest:
                mult = cols[b][j] * scale
                if b == kb:
                    mult = jnp.where(sub8 >= kr + GROUP, mult, 0.0)
                blocks[b] = blocks[b] - mult * rows[j]
                for l in range(j + 1, GROUP):
                    cols[b][l] = cols[b][l] - cols[b][j] * ratio[l]
    lower = jnp.concatenate(done, axis=0)
    return dot(
        lower, jnp.concatenate([zeros, wt, zeros, zeros], axis=0), NN, lax.Precision.HIGHEST
    )


def basis_kernel(
    sizes,
    fields,
    start,
    vt_out,
    core_out,
    faces_out,
    halo_out,
    cells,
    picked,
    snap,
    edges,
    face_src,
    send_buf,
    recv_buf,
    piece_buf,
    cross_buf,
    whole_buf,
    load_sem,
    rs_send,
    rs_recv,
    ag_send,
    ag_recv,
    cr_send,
    cr_recv,
    face_send,
    face_recv,
    halo_send,
    halo_recv,
):
    nb, ns, total = sizes
    blk = lax.axis_index("blk")
    sub = lax.axis_index("sub")
    me = blk * ns + sub
    devices = nb * ns
    groups = devices // PIECES
    team, place = me // PIECES, me % PIECES
    nvar, bx, cy, bz = cells.shape
    mode = snap.shape[1]

    def where_is(index):
        return (index // ns, index % ns)

    loads = [
        pltpu.make_async_copy(fields.at[v], cells.at[v], load_sem.at[v]) for v in range(nvar)
    ]
    for load in loads:
        load.start()

    barrier = pltpu.get_barrier_semaphore()

    @pl.loop(1, devices)
    def _(k):
        pl.semaphore_signal(
            barrier, inc=1, device_id=where_is((me + k) % devices), device_id_type=MESH
        )

    vt = jnp.transpose(start[...])
    pick = (
        lax.broadcasted_iota(jnp.int32, (256, 128), 0)
        == 2 * lax.broadcasted_iota(jnp.int32, (256, 128), 1)
    ).astype(F32).astype(BF16)
    pick_rows = (
        lax.broadcasted_iota(jnp.int32, (128, 256), 1)
        == 2 * lax.broadcasted_iota(jnp.int32, (128, 256), 0)
    ).astype(F32).astype(BF16)
    for v in range(nvar):
        loads[v].wait()
        for xe in range(bx // 2):
            at = (v * (bx // 2) + xe) * cy
            picked[at : at + cy, :] = (cells[v, 2 * xe] - LEVELS[v]).astype(BF16)
    for h in range(2):
        for j in range(mode // 128):
            part = dot(
                picked[256 * h : 256 * h + 256, 256 * j : 256 * j + 256], pick, NN
            ).astype(BF16)
            snap[128 * h : 128 * h + 128, 128 * j : 128 * j + 128] = dot(
                pick_rows, part, NN
            ).astype(BF16)

    inv_total = 1.0 / total
    for it in range(ITERS):
        partial = join3(dot(split3(vt), snap[...], NT)) * inv_total
        partial = join3(dot(split3(partial), snap[...], NN))
        for g in range(8):
            for j in range(4):
                send_buf[it, g * 4 + j] = partial[4 * g : 4 * g + 4, 128 * j : 128 * j + 128]
        if it == 0:
            pl.semaphore_wait(barrier, devices - 1)

        @pl.loop(1, PIECES)
        def _(k):
            other = (place + k) % PIECES
            pltpu.make_async_remote_copy(
                src_ref=send_buf.at[it, other],
                dst_ref=recv_buf.at[it, place],
                send_sem=rs_send.at[it],
                recv_sem=rs_recv.at[it],
                device_id=where_is(team * PIECES + other),
                device_id_type=MESH,
            ).start()

        recv_buf[it, pl.ds(place, 1)] = send_buf[it, pl.ds(place, 1)]

        if it == 0:
            lane = lax.broadcasted_iota(jnp.int32, (cy, 128), 1)
            face = jnp.zeros((cy, 128), F32)
            for v in range(nvar):
                for x in range(bx):
                    low = jnp.broadcast_to(cells[v, x, :, 0:128][:, 0:1], (cy, 128))
                    high = jnp.broadcast_to(
                        cells[v, x, :, bz - 128 : bz][:, 127:128], (cy, 128)
                    )
                    face = jnp.where(lane == v * bx + x, low, face)
                    face = jnp.where(lane == 64 + v * bx + x, high, face)
            face_src[...] = face
            faces_out[pl.ds(blk, 1)] = face[None]

            @pl.loop(1, nb)
            def _(k):
                pltpu.make_async_remote_copy(
                    src_ref=face_src,
                    dst_ref=faces_out.at[blk],
                    send_sem=face_send,
                    recv_sem=face_recv,
                    device_id=((blk + k) % nb, sub),
                    device_id_type=MESH,
                ).start()

            for v in range(nvar):
                edges[0, v] = cells[v, :, 0, :]
                edges[1, v] = cells[v, :, cy - 1, :]

        landed = recv_buf.at[it, pl.ds(0, PIECES - 1)]
        pltpu.make_async_copy(landed, landed, rs_recv.at[it]).wait()
        piece = jnp.sum(recv_buf[it], axis=0)
        if groups > 1:
            piece_buf[it, 0] = piece
            cross_buf[it, pl.ds(team, 1)] = piece[None]

            @pl.loop(1, groups)
            def _(k):
                pltpu.make_async_remote_copy(
                    src_ref=piece_buf.at[it, 0],
                    dst_ref=cross_buf.at[it, team],
                    send_sem=cr_send.at[it],
                    recv_sem=cr_recv.at[it],
                    device_id=where_is(((team + k) % groups) * PIECES + place),
                    device_id_type=MESH,
                ).start()

            crossed = cross_buf.at[it, pl.ds(0, groups - 1)]
            pltpu.make_async_copy(crossed, crossed, cr_recv.at[it]).wait()
            piece = jnp.sum(cross_buf[it], axis=0)
        piece_buf[it, 1] = piece
        whole_buf[it, pl.ds(place, 1)] = piece[None]

        @pl.loop(1, PIECES)
        def _(k):
            pltpu.make_async_remote_copy(
                src_ref=piece_buf.at[it, 1],
                dst_ref=whole_buf.at[it, place],
                send_sem=ag_send.at[it],
                recv_sem=ag_recv.at[it],
                device_id=where_is(team * PIECES + (place + k) % PIECES),
                device_id_type=MESH,
            ).start()

        gathered = whole_buf.at[it, pl.ds(0, PIECES - 1)]
        pltpu.make_async_copy(gathered, gathered, ag_recv.at[it]).wait()
        for side, step in ((0, ns - 1), (1, 1)):
            pltpu.make_async_remote_copy(
                src_ref=edges.at[side, it],
                dst_ref=halo_out.at[side, it],
                send_sem=halo_send.at[side, it],
                recv_sem=halo_recv.at[side, it],
                device_id=(blk, (sub + step) % ns),
                device_id_type=MESH,
            ).start()
        wt = jnp.concatenate(
            [
                jnp.concatenate([whole_buf[it, g * 4 + j] for j in range(4)], axis=1)
                for g in range(8)
            ],
            axis=0,
        )
        vt = factor_apply(wt)

    vt_out[...] = vt
    core_out[...] = join3(dot(split3(vt), snap[...], NT)) * (1.0 / math.sqrt(mode))

    for it in range(ITERS):
        landed = recv_buf.at[it, pl.ds(0, PIECES - 1)]
        pltpu.make_async_copy(landed, landed, rs_send.at[it]).wait()
        pltpu.make_async_copy(landed, landed, ag_send.at[it]).wait()
        if groups > 1:
            crossed = cross_buf.at[it, pl.ds(0, groups - 1)]
            pltpu.make_async_copy(crossed, crossed, cr_send.at[it]).wait()
        for side in range(2):
            pltpu.make_async_copy(
                edges.at[side, it], edges.at[side, it], halo_send.at[side, it]
            ).wait()
            pltpu.make_async_copy(
                halo_out.at[side, it], halo_out.at[side, it], halo_recv.at[side, it]
            ).wait()
    gathered = faces_out.at[pl.ds(0, nb - 1)]
    pltpu.make_async_copy(gathered, gathered, face_send).wait()
    pltpu.make_async_copy(gathered, gathered, face_recv).wait()


def section_kernel(
    nb, slots, links, bases, fractions, speeds, fields, faces, halo, out, penalty, cells, made,
    load_sem, store_sem
):
    nvar, bx, cy, bz = cells.shape
    for_x = [bx - 1, 0, 1] + list(range(2, bx - 1))
    loads = [
        pltpu.make_async_copy(fields.at[:, x], cells.at[:, x], load_sem.at[x]) for x in range(bx)
    ]
    for x in for_x:
        loads[x].start()
    my_slot = lax.axis_index("blk")
    speed = speeds[0]
    mine = lax.fori_loop(
        0, nb, lambda b, acc: jnp.where(slots[b] == my_slot, b, acc), jnp.int32(0)
    )
    upstream = faces[slots[links[mine, 0]]]
    downstream = faces[slots[links[mine, 1]]]
    own = faces[my_slot]
    lane = lax.broadcasted_iota(jnp.int32, (1, 128), 1)
    node = jnp.zeros((1, 128), jnp.int32)
    frac = jnp.zeros((1, 128), F32)
    for s in range(2):
        for x in range(bx):
            here = (lane // 64 == s) & (lane % 16 == x)
            node = jnp.where(here, bases[mine, s, x], node)
            frac = jnp.where(here, fractions[mine, s, x], frac)
    square_row = lax.broadcasted_iota(jnp.int32, (128, 128), 0)
    square_lane = lax.broadcasted_iota(jnp.int32, (128, 128), 1)
    given = square_row % 16
    weights = jnp.where(given == node, 1.0 - frac, 0.0) + jnp.where(
        given == (node + 1) % bx, frac, 0.0
    )
    weights = jnp.where(square_row // 16 == square_lane // 16, weights, 0.0)
    lane16 = lax.broadcasted_iota(jnp.int32, (cy, 128), 1)
    donors = pltpu.roll(jnp.where(lane16 < 64, downstream, upstream), 64, 1)
    inflow = dot(donors, weights, NN, lax.Precision.HIGHEST)
    low_factor = -2.0 * (speed + DIFFUSIVITY)
    factor = jnp.where(lane16 < 64, low_factor, -2.0 * DIFFUSIVITY)
    pen = factor * (own - inflow)
    penalty[...] = jnp.transpose(pen)

    first = lane16 == 0
    last = lane16 == 127
    row = lax.broadcasted_iota(jnp.int32, (cy, bz), 0)
    stores = [
        pltpu.make_async_copy(made.at[:, x], out.at[:, x], store_sem.at[x]) for x in range(bx)
    ]
    loads[bx - 1].wait()
    loads[0].wait()
    for x in range(bx):
        if x + 1 < bx - 1:
            loads[x + 1].wait()
        rate = (
            PREFACTOR * cells[1, x] * cells[2, x] * jnp.exp(-ACTIVATION / cells[0, x])
        )
        for v in range(nvar):
            f = cells[v, x]
            around = cells[v, (x + 1) % bx] + cells[v, (x - 1) % bx]
            ahead_y = jnp.where(row == cy - 1, halo[0, v, x : x + 1, :], pltpu.roll(f, cy - 1, 0))
            behind_y = jnp.where(row == 0, halo[1, v, x : x + 1, :], pltpu.roll(f, 1, 0))
            ahead = pltpu.roll(f, bz - 1, 1)
            behind = pltpu.roll(f, 1, 1)
            slope = (ahead - behind) * 0.5
            around = (around + ahead_y + behind_y) - 4.0 * f
            curve = (ahead - 2.0 * f) + behind
            source = (HEAT_RELEASE, -1.0, -OXIDIZER_RATIO, 1.0 + OXIDIZER_RATIO)[v] * rate
            base = DIFFUSIVITY * around + source
            along = DIFFUSIVITY * curve - speed * slope
            made[v, x] = f + TIME_STEP * (base + along)
            at = v * bx + x
            f0 = f[:, 0:128]
            f1 = pltpu.roll(f0, 127, 1)
            f2 = pltpu.roll(f0, 126, 1)
            edge = DIFFUSIVITY * ((f0 - 2.0 * f1) + f2) - speed * (f1 - f0) + pen[:, at : at + 1]
            made[v, x, :, 0:128] = f0 + TIME_STEP * (
                base[:, 0:128] + jnp.where(first, edge, along[:, 0:128])
            )
            f0 = f[:, bz - 128 : bz]
            f1 = pltpu.roll(f0, 1, 1)
            f2 = pltpu.roll(f0, 2, 1)
            edge = (
                DIFFUSIVITY * ((f0 - 2.0 * f1) + f2)
                - speed * (f0 - f1)
                + pen[:, 64 + at : 65 + at]
            )
            made[v, x, :, bz - 128 : bz] = f0 + TIME_STEP * (
                base[:, bz - 128 : bz] + jnp.where(last, edge, along[:, bz - 128 : bz])
            )
        stores[x].start()
    for store in stores:
        store.wait()


def per_device(nb, ns, fields, block_speed, neighbours, block_slot, table_base, table_weight, start_basis):
    local = fields[0]
    nvar, bx, cy, bz = local.shape
    mode, rank = start_basis.shape
    rows = nvar * (bx // 2) * (cy // 2)
    groups = nb * ns // PIECES
    vmem = pl.BlockSpec(memory_space=pltpu.VMEM)
    smem = pl.BlockSpec(memory_space=pltpu.SMEM)
    anywhere = pl.BlockSpec(memory_space=pl.ANY)
    dma = pltpu.SemaphoreType.DMA
    vt, core, faces, halo = pl.pallas_call(
        functools.partial(basis_kernel, (nb, ns, rows * nb * ns)),
        out_shape=(
            jax.ShapeDtypeStruct((rank, mode), F32),
            jax.ShapeDtypeStruct((rank, rows), F32),
            jax.ShapeDtypeStruct((nb, cy, 128), F32),
            jax.ShapeDtypeStruct((2, nvar, bx, bz), F32),
        ),
        in_specs=[anywhere, vmem],
        out_specs=(vmem, vmem, vmem, vmem),
        scratch_shapes=[
            pltpu.VMEM((nvar, bx, cy, bz), F32),
            pltpu.VMEM((2 * rows, bz), BF16),
            pltpu.VMEM((rows, mode), BF16),
            pltpu.VMEM((2, nvar, bx, bz), F32),
            pltpu.VMEM((cy, 128), F32),
            pltpu.VMEM((ITERS, PIECES, 4, 128), F32),
            pltpu.VMEM((ITERS, PIECES, 4, 128), F32),
            pltpu.VMEM((ITERS, 2, 4, 128), F32),
            pltpu.VMEM((ITERS, max(groups, 2), 4, 128), F32),
            pltpu.VMEM((ITERS, PIECES, 4, 128), F32),
            dma((nvar,)),
            dma((ITERS,)),
            dma((ITERS,)),
            dma((ITERS,)),
            dma((ITERS,)),
            dma((ITERS,)),
            dma((ITERS,)),
            dma,
            dma,
            dma((2, ITERS)),
            dma((2, ITERS)),
        ],
        compiler_params=pltpu.CompilerParams(
            collective_id=0, has_side_effects=True, vmem_limit_bytes=40 * 1024 * 1024
        ),
        name="basis",
    )(local, start_basis)
    section, penalty = pl.pallas_call(
        functools.partial(section_kernel, nb),
        out_shape=(
            jax.ShapeDtypeStruct((nvar, bx, cy, bz), F32),
            jax.ShapeDtypeStruct((128, cy), F32),
        ),
        in_specs=[smem, smem, smem, smem, smem, anywhere, vmem, vmem],
        out_specs=(anywhere, vmem),
        scratch_shapes=[
            pltpu.VMEM((nvar, bx, cy, bz), F32),
            pltpu.VMEM((nvar, bx, cy, bz), F32),
            dma((bx,)),
            dma((bx,)),
        ],
        compiler_params=pltpu.CompilerParams(vmem_limit_bytes=40 * 1024 * 1024),
        name="section",
    )(block_slot, neighbours, table_base, table_weight, block_speed, local, faces, halo)
    return (
        section[None],
        penalty.reshape(1, 2, nvar, bx, cy),
        vt.T,
        core,
    )


def solution(mesh):
    in_specs = (P("blk", None, None, "sub", None), P("blk"), P(), P(), P(), P(), P())
    out_specs = (
        P("blk", None, None, "sub", None),
        P("blk", None, None, None, "sub"),
        P(),
        P(None, ("blk", "sub")),
    )
    body = functools.partial(per_device, mesh.shape["blk"], mesh.shape["sub"])
    return jax.shard_map(
        body, mesh=mesh, in_specs=in_specs, out_specs=out_specs, check_vma=False
    )
```

```python
import functools
import math

import jax
import jax.numpy as jnp
from jax import lax
from jax.experimental import pallas as pl
from jax.experimental.pallas import tpu as pltpu
from jax.sharding import PartitionSpec as P

ITERS = 4
LEVELS = (2.0, 0.525, 0.525, 0.525)
PIECES = 32
GROUP = 8
TIME_STEP = 0.1
DIFFUSIVITY = 0.5
PREFACTOR = 5.0
ACTIVATION = 4.0
HEAT_RELEASE = 2.0
OXIDIZER_RATIO = 1.5
F32 = jnp.float32
BF16 = jnp.bfloat16
MESH = pl.DeviceIdType.MESH
NT = (((1,), (1,)), ((), ()))
NN = (((1,), (0,)), ((), ()))


def dot(a, b, dims, precision=None):
    return lax.dot_general(a, b, dims, precision=precision, preferred_element_type=F32)


def split3(a):
    high = a.astype(BF16)
    rest = a - high.astype(F32)
    mid = rest.astype(BF16)
    low = (rest - mid.astype(F32)).astype(BF16)
    return jnp.concatenate([high, mid, low], axis=0)


def join3(a):
    n = a.shape[0] // 3
    return (a[2 * n :] + a[n : 2 * n]) + a[:n]


def factor_apply(wt):
    rank, mode = wt.shape
    zeros = jnp.zeros((rank, mode), F32)
    inner = dot(
        wt, jnp.concatenate([wt, zeros, zeros, zeros], axis=0), NT, lax.Precision.HIGHEST
    )
    row = lax.broadcasted_iota(jnp.int32, (rank, 128), 0)
    lane = lax.broadcasted_iota(jnp.int32, (rank, 128), 1)
    inner = inner + jnp.where(lane == row + rank, 1.0, 0.0)
    blocks = [inner[8 * i : 8 * i + 8] for i in range(rank // 8)]
    sub8 = lax.broadcasted_iota(jnp.int32, (8, 128), 0)
    full = (8, 128)
    done = [jnp.zeros(full, F32) for _ in blocks]
    for k in range(0, rank, GROUP):
        kb, kr = k // 8, k % 8
        rows = [
            jnp.broadcast_to(blocks[kb][kr + l : kr + l + 1], full) for l in range(GROUP)
        ]
        elem = [
            [
                jnp.broadcast_to(rows[l][:, k + j : k + j + 1], full) if j >= l else None
                for j in range(GROUP)
            ]
            for l in range(GROUP)
        ]
        rest = [b for b in range(kb, len(blocks)) if b > kb or kr + GROUP < 8]
        cols = {
            b: [jnp.broadcast_to(blocks[b][:, k + j : k + j + 1], full) for j in range(GROUP)]
            for b in rest
        }
        for j in range(GROUP):
            scale = 1.0 / elem[j][j]
            root = lax.rsqrt(elem[j][j])
            done[kb] = jnp.where(sub8 == kr + j, rows[j] * root, done[kb])
            ratio = [
                elem[j][l] * scale if l > j else None for l in range(GROUP)
            ]
            for l in range(j + 1, GROUP):
                rows[l] = rows[l] - ratio[l] * rows[j]
                for m in range(l, GROUP):
                    elem[l][m] = elem[l][m] - ratio[l] * elem[j][m]
            for b in rest:
                mult = cols[b][j] * scale
                if b == kb:
                    mult = jnp.where(sub8 >= kr + GROUP, mult, 0.0)
                blocks[b] = blocks[b] - mult * rows[j]
                for l in range(j + 1, GROUP):
                    cols[b][l] = cols[b][l] - cols[b][j] * ratio[l]
    lower = jnp.concatenate(done, axis=0)
    return dot(
        lower, jnp.concatenate([zeros, wt, zeros, zeros], axis=0), NN, lax.Precision.HIGHEST
    )


def face_penalty(nb, my_slot, slots, links, bases, fractions, speeds, faces, pens, penalty):
    bx = 16
    cy = pens.shape[0]
    mine = lax.fori_loop(
        0, nb, lambda b, acc: jnp.where(slots[b] == my_slot, b, acc), jnp.int32(0)
    )
    upstream = faces[slots[links[0, mine]]]
    downstream = faces[slots[links[1, mine]]]
    own = faces[my_slot]
    lane = lax.broadcasted_iota(jnp.int32, (1, 128), 1)
    node = jnp.zeros((1, 128), jnp.int32)
    frac = jnp.zeros((1, 128), F32)
    for s in range(2):
        for x in range(bx):
            here = (lane // 64 == s) & (lane % bx == x)
            node = jnp.where(here, bases[mine, s, x], node)
            frac = jnp.where(here, fractions[mine, s, x], frac)
    square_row = lax.broadcasted_iota(jnp.int32, (128, 128), 0)
    square_lane = lax.broadcasted_iota(jnp.int32, (128, 128), 1)
    given = square_row % bx
    after = jnp.where(node == bx - 1, 0, node + 1)
    weights = jnp.where(given == node, 1.0 - frac, 0.0) + jnp.where(given == after, frac, 0.0)
    weights = jnp.where(square_row // bx == square_lane // bx, weights, 0.0)
    wide = lax.broadcasted_iota(jnp.int32, (cy, 128), 1)
    donors = pltpu.roll(jnp.where(wide < 64, downstream, upstream), 64, 1)
    inflow = dot(donors, weights, NN, lax.Precision.HIGHEST)
    factor = jnp.where(wide < 64, -2.0 * (speeds[0] + DIFFUSIVITY), -2.0 * DIFFUSIVITY)
    pen = factor * (own - inflow)
    pens[...] = pen
    penalty[...] = jnp.transpose(pen)


def section_rows(v, speed, cells, halo, rates, pens, made):
    nvar, bx, cy, bz = cells.shape
    lane = lax.broadcasted_iota(jnp.int32, (cy, 128), 1)
    row = lax.broadcasted_iota(jnp.int32, (cy, bz), 0)
    factor = (HEAT_RELEASE, -1.0, -OXIDIZER_RATIO, 1.0 + OXIDIZER_RATIO)[v]

    @pl.loop(0, bx, unroll=2)
    def _(x):
        f = cells[v, x]
        around = cells[v, (x + 1) % bx] + cells[v, (x + bx - 1) % bx]
        ahead_y = jnp.where(row == cy - 1, halo[0, v, pl.ds(x, 1), :], pltpu.roll(f, cy - 1, 0))
        behind_y = jnp.where(row == 0, halo[1, v, pl.ds(x, 1), :], pltpu.roll(f, 1, 0))
        ahead = pltpu.roll(f, bz - 1, 1)
        behind = pltpu.roll(f, 1, 1)
        slope = (ahead - behind) * 0.5
        around = (around + ahead_y + behind_y) - 4.0 * f
        curve = (ahead - 2.0 * f) + behind
        base = DIFFUSIVITY * around + factor * rates[x]
        along = DIFFUSIVITY * curve - speed * slope
        made[v, x] = f + TIME_STEP * (base + along)
        at = v * bx + x
        pen = pens[...]
        low = jnp.sum(jnp.where(lane == at, pen, 0.0), axis=1, keepdims=True)
        high = jnp.sum(jnp.where(lane == at + 64, pen, 0.0), axis=1, keepdims=True)
        f0 = f[:, 0:128]
        f1 = pltpu.roll(f0, 127, 1)
        f2 = pltpu.roll(f0, 126, 1)
        edge = DIFFUSIVITY * ((f0 - 2.0 * f1) + f2) - speed * (f1 - f0) + low
        made[v, x, :, 0:128] = f0 + TIME_STEP * (
            base[:, 0:128] + jnp.where(lane == 0, edge, along[:, 0:128])
        )
        f0 = f[:, bz - 128 : bz]
        f1 = pltpu.roll(f0, 1, 1)
        f2 = pltpu.roll(f0, 2, 1)
        edge = DIFFUSIVITY * ((f0 - 2.0 * f1) + f2) - speed * (f0 - f1) + high
        made[v, x, :, bz - 128 : bz] = f0 + TIME_STEP * (
            base[:, bz - 128 : bz] + jnp.where(lane == 127, edge, along[:, bz - 128 : bz])
        )


def finish_kernel(made, penalty, vt, snap, out, penalty_out, vt_out, core_out, store_sem):
    store = pltpu.make_async_copy(made, out, store_sem)
    store.start()
    mode = vt.shape[1]
    penalty_out[...] = penalty[...]
    vt_out[...] = vt[...]
    core_out[...] = join3(dot(split3(vt[...]), snap[...], NT)) * (1.0 / math.sqrt(mode))
    store.wait()


def basis_kernel(
    sizes,
    slots,
    links,
    bases,
    fractions,
    speeds,
    fields,
    start,
    vt_out,
    snap,
    made,
    penalty,
    cells,
    picked,
    rates,
    pens,
    faces_in,
    halo,
    edges,
    face_src,
    send_buf,
    recv_buf,
    piece_buf,
    cross_buf,
    whole_buf,
    load_sem,
    rs_send,
    rs_recv,
    ag_send,
    ag_recv,
    cr_send,
    cr_recv,
    face_send,
    face_recv,
    halo_send,
    halo_recv,
):
    nb, ns, total = sizes
    blk = lax.axis_index("blk")
    sub = lax.axis_index("sub")
    me = blk * ns + sub
    devices = nb * ns
    groups = devices // PIECES
    team, place = me // PIECES, me % PIECES
    nvar, bx, cy, bz = cells.shape
    mode = snap.shape[1]

    def where_is(index):
        return (index // ns, index % ns)

    loads = [
        pltpu.make_async_copy(fields.at[v], cells.at[v], load_sem.at[v]) for v in range(nvar)
    ]
    for load in loads:
        load.start()

    barrier = pltpu.get_barrier_semaphore()

    @pl.loop(1, devices)
    def _(k):
        pl.semaphore_signal(
            barrier, inc=1, device_id=where_is((me + k) % devices), device_id_type=MESH
        )

    vt = start[...]
    pick = (
        lax.broadcasted_iota(jnp.int32, (256, 128), 0)
        == 2 * lax.broadcasted_iota(jnp.int32, (256, 128), 1)
    ).astype(F32).astype(BF16)
    pick_rows = (
        lax.broadcasted_iota(jnp.int32, (128, 256), 1)
        == 2 * lax.broadcasted_iota(jnp.int32, (128, 256), 0)
    ).astype(F32).astype(BF16)
    for v in range(nvar):
        loads[v].wait()
        for xe in range(bx // 2):
            at = (v * (bx // 2) + xe) * cy
            picked[at : at + cy, :] = (cells[v, 2 * xe] - LEVELS[v]).astype(BF16)
    for h in range(2):
        for j in range(mode // 128):
            part = dot(
                picked[256 * h : 256 * h + 256, 256 * j : 256 * j + 256], pick, NN
            ).astype(BF16)
            snap[128 * h : 128 * h + 128, 128 * j : 128 * j + 128] = dot(
                pick_rows, part, NN
            ).astype(BF16)

    def send_faces():
        lane = lax.broadcasted_iota(jnp.int32, (cy, 128), 1)
        face = jnp.zeros((cy, 128), F32)
        for v in range(nvar):
            for x in range(bx):
                low = jnp.broadcast_to(cells[v, x, :, 0:128][:, 0:1], (cy, 128))
                high = jnp.broadcast_to(
                    cells[v, x, :, bz - 128 : bz][:, 127:128], (cy, 128)
                )
                face = jnp.where(lane == v * bx + x, low, face)
                face = jnp.where(lane == 64 + v * bx + x, high, face)
        face_src[...] = face
        faces_in[pl.ds(blk, 1)] = face[None]

        @pl.loop(1, nb)
        def _(k):
            pltpu.make_async_remote_copy(
                src_ref=face_src,
                dst_ref=faces_in.at[blk],
                send_sem=face_send,
                recv_sem=face_recv,
                device_id=((blk + k) % nb, sub),
                device_id_type=MESH,
            ).start()

        for v in range(nvar):
            edges[0, v] = cells[v, :, 0, :]
            edges[1, v] = cells[v, :, cy - 1, :]

    def send_edges(v):
        for side, step in ((0, ns - 1), (1, 1)):
            pltpu.make_async_remote_copy(
                src_ref=edges.at[side, v],
                dst_ref=halo.at[side, v],
                send_sem=halo_send.at[side, v],
                recv_sem=halo_recv.at[side, v],
                device_id=(blk, (sub + step) % ns),
                device_id_type=MESH,
            ).start()

    def build_rates():
        @pl.loop(0, bx)
        def _(x):
            rates[x] = PREFACTOR * cells[1, x] * cells[2, x] * jnp.exp(-ACTIVATION / cells[0, x])

    def build_penalty():
        landed = faces_in.at[pl.ds(0, nb - 1)]
        pltpu.make_async_copy(landed, landed, face_recv).wait()
        face_penalty(nb, blk, slots, links, bases, fractions, speeds, faces_in, pens, penalty)

    def build_section(v):
        for side in range(2):
            landed = halo.at[side, v]
            pltpu.make_async_copy(landed, landed, halo_recv.at[side, v]).wait()
        section_rows(v, speeds[0], cells, halo, rates, pens, made)

    def fill(slot):
        if slot == 0:
            send_faces()
        if slot < 4:
            send_edges(slot)
        if slot == 1:
            build_rates()
        if slot == 2:
            build_penalty()
        if 3 <= slot < 3 + nvar:
            build_section(slot - 3)

    inv_total = 1.0 / total
    for it in range(ITERS):
        partial = join3(dot(split3(vt), snap[...], NT)) * inv_total
        partial = join3(dot(split3(partial), snap[...], NN))
        for g in range(8):
            for j in range(4):
                send_buf[it, g * 4 + j] = partial[4 * g : 4 * g + 4, 128 * j : 128 * j + 128]
        if it == 0:
            pl.semaphore_wait(barrier, devices - 1)

        @pl.loop(1, PIECES)
        def _(k):
            other = (place + k) % PIECES
            pltpu.make_async_remote_copy(
                src_ref=send_buf.at[it, other],
                dst_ref=recv_buf.at[it, place],
                send_sem=rs_send.at[it],
                recv_sem=rs_recv.at[it],
                device_id=where_is(team * PIECES + other),
                device_id_type=MESH,
            ).start()

        recv_buf[it, pl.ds(place, 1)] = send_buf[it, pl.ds(place, 1)]

        fill(2 * it)
        landed = recv_buf.at[it, pl.ds(0, PIECES - 1)]
        pltpu.make_async_copy(landed, landed, rs_recv.at[it]).wait()
        piece = jnp.sum(recv_buf[it], axis=0)
        if groups > 1:
            piece_buf[it, 0] = piece
            cross_buf[it, pl.ds(team, 1)] = piece[None]

            @pl.loop(1, groups)
            def _(k):
                pltpu.make_async_remote_copy(
                    src_ref=piece_buf.at[it, 0],
                    dst_ref=cross_buf.at[it, team],
                    send_sem=cr_send.at[it],
                    recv_sem=cr_recv.at[it],
                    device_id=where_is(((team + k) % groups) * PIECES + place),
                    device_id_type=MESH,
                ).start()

            crossed = cross_buf.at[it, pl.ds(0, groups - 1)]
            pltpu.make_async_copy(crossed, crossed, cr_recv.at[it]).wait()
            piece = jnp.sum(cross_buf[it], axis=0)
        piece_buf[it, 1] = piece
        whole_buf[it, pl.ds(place, 1)] = piece[None]

        @pl.loop(1, PIECES)
        def _(k):
            pltpu.make_async_remote_copy(
                src_ref=piece_buf.at[it, 1],
                dst_ref=whole_buf.at[it, place],
                send_sem=ag_send.at[it],
                recv_sem=ag_recv.at[it],
                device_id=where_is(team * PIECES + (place + k) % PIECES),
                device_id_type=MESH,
            ).start()

        fill(2 * it + 1)
        gathered = whole_buf.at[it, pl.ds(0, PIECES - 1)]
        pltpu.make_async_copy(gathered, gathered, ag_recv.at[it]).wait()
        wt = jnp.concatenate(
            [
                jnp.concatenate([whole_buf[it, g * 4 + j] for j in range(4)], axis=1)
                for g in range(8)
            ],
            axis=0,
        )
        vt = factor_apply(wt)

    vt_out[...] = vt

    for it in range(ITERS):
        landed = recv_buf.at[it, pl.ds(0, PIECES - 1)]
        pltpu.make_async_copy(landed, landed, rs_send.at[it]).wait()
        pltpu.make_async_copy(landed, landed, ag_send.at[it]).wait()
        if groups > 1:
            crossed = cross_buf.at[it, pl.ds(0, groups - 1)]
            pltpu.make_async_copy(crossed, crossed, cr_send.at[it]).wait()
        for side in range(2):
            pltpu.make_async_copy(
                edges.at[side, it], edges.at[side, it], halo_send.at[side, it]
            ).wait()
    gathered = faces_in.at[pl.ds(0, nb - 1)]
    pltpu.make_async_copy(gathered, gathered, face_send).wait()


def per_device(nb, ns, fields, block_speed, neighbours, block_slot, table_base, table_weight, start_basis):
    local = fields[0]
    nvar, bx, cy, bz = local.shape
    mode, rank = start_basis.shape
    rows = nvar * (bx // 2) * (cy // 2)
    groups = nb * ns // PIECES
    vmem = pl.BlockSpec(memory_space=pltpu.VMEM)
    smem = pl.BlockSpec(memory_space=pltpu.SMEM)
    dma = pltpu.SemaphoreType.DMA
    vt, snap, made, penalty = pl.pallas_call(
        functools.partial(basis_kernel, (nb, ns, rows * nb * ns)),
        out_shape=(
            jax.ShapeDtypeStruct((rank, mode), F32),
            jax.ShapeDtypeStruct((rows, mode), BF16),
            jax.ShapeDtypeStruct((nvar, bx, cy, bz), F32),
            jax.ShapeDtypeStruct((128, cy), F32),
        ),
        in_specs=[smem] * 5 + [pl.BlockSpec(memory_space=pltpu.HBM), vmem],
        out_specs=(vmem, vmem, vmem, vmem),
        scratch_shapes=[
            pltpu.VMEM((nvar, bx, cy, bz), F32),
            pltpu.VMEM((2 * rows, bz), BF16),
            pltpu.VMEM((bx, cy, bz), F32),
            pltpu.VMEM((cy, 128), F32),
            pltpu.VMEM((nb, cy, 128), F32),
            pltpu.VMEM((2, nvar, bx, bz), F32),
            pltpu.VMEM((2, nvar, bx, bz), F32),
            pltpu.VMEM((cy, 128), F32),
            pltpu.VMEM((ITERS, PIECES, 4, 128), F32),
            pltpu.VMEM((ITERS, PIECES, 4, 128), F32),
            pltpu.VMEM((ITERS, 2, 4, 128), F32),
            pltpu.VMEM((ITERS, max(groups, 2), 4, 128), F32),
            pltpu.VMEM((ITERS, PIECES, 4, 128), F32),
            dma((nvar,)),
            dma((ITERS,)),
            dma((ITERS,)),
            dma((ITERS,)),
            dma((ITERS,)),
            dma((ITERS,)),
            dma((ITERS,)),
            dma,
            dma,
            dma((2, ITERS)),
            dma((2, ITERS)),
        ],
        compiler_params=pltpu.CompilerParams(
            collective_id=0, has_side_effects=True, vmem_limit_bytes=40 * 1024 * 1024
        ),
        name="basis",
    )(block_slot, neighbours.T, table_base, table_weight, block_speed, local, start_basis.T)
    section, penalty, vt, core = pl.pallas_call(
        finish_kernel,
        out_shape=(
            jax.ShapeDtypeStruct((nvar, bx, cy, bz), F32),
            jax.ShapeDtypeStruct((128, cy), F32),
            jax.ShapeDtypeStruct((rank, mode), F32),
            jax.ShapeDtypeStruct((rank, rows), F32),
        ),
        in_specs=[vmem] * 4,
        out_specs=(pl.BlockSpec(memory_space=pltpu.HBM), vmem, vmem, vmem),
        scratch_shapes=[dma],
        name="finish",
    )(made, penalty, vt, snap)
    return (
        section[None],
        penalty.reshape(1, 2, nvar, bx, cy),
        vt.T,
        core,
    )


def solution(mesh):
    in_specs = (P("blk", None, None, "sub", None), P("blk"), P(), P(), P(), P(), P())
    out_specs = (
        P("blk", None, None, "sub", None),
        P("blk", None, None, None, "sub"),
        P(),
        P(None, ("blk", "sub")),
    )
    body = functools.partial(per_device, mesh.shape["blk"], mesh.shape["sub"])
    return jax.shard_map(
        body, mesh=mesh, in_specs=in_specs, out_specs=out_specs, check_vma=False
    )
```

```python
import functools
import math

import jax
import jax.numpy as jnp
from jax import lax
from jax.experimental import pallas as pl
from jax.experimental.pallas import tpu as pltpu
from jax.sharding import PartitionSpec as P

ITERS = 4
LEVELS = (2.0, 0.525, 0.525, 0.525)
PIECES = 32
GROUP = 8
TIME_STEP = 0.1
DIFFUSIVITY = 0.5
PREFACTOR = 5.0
ACTIVATION = 4.0
HEAT_RELEASE = 2.0
OXIDIZER_RATIO = 1.5
F32 = jnp.float32
BF16 = jnp.bfloat16
MESH = pl.DeviceIdType.MESH
NT = (((1,), (1,)), ((), ()))
NN = (((1,), (0,)), ((), ()))


def dot(a, b, dims, precision=None):
    return lax.dot_general(a, b, dims, precision=precision, preferred_element_type=F32)


def split3(a):
    high = a.astype(BF16)
    rest = a - high.astype(F32)
    mid = rest.astype(BF16)
    low = (rest - mid.astype(F32)).astype(BF16)
    return jnp.concatenate([high, mid, low], axis=0)


def join3(a):
    n = a.shape[0] // 3
    return (a[2 * n :] + a[n : 2 * n]) + a[:n]


def factor_apply(wt):
    rank, mode = wt.shape
    zeros = jnp.zeros((rank, mode), F32)
    inner = dot(
        wt, jnp.concatenate([wt, zeros, zeros, zeros], axis=0), NT, lax.Precision.HIGHEST
    )
    row = lax.broadcasted_iota(jnp.int32, (rank, 128), 0)
    lane = lax.broadcasted_iota(jnp.int32, (rank, 128), 1)
    inner = inner + jnp.where(lane == row + rank, 1.0, 0.0)
    blocks = [inner[8 * i : 8 * i + 8] for i in range(rank // 8)]
    sub8 = lax.broadcasted_iota(jnp.int32, (8, 128), 0)
    full = (8, 128)
    done = [jnp.zeros(full, F32) for _ in blocks]
    for k in range(0, rank, GROUP):
        kb, kr = k // 8, k % 8
        rows = [
            jnp.broadcast_to(blocks[kb][kr + l : kr + l + 1], full) for l in range(GROUP)
        ]
        elem = [
            [
                jnp.broadcast_to(rows[l][:, k + j : k + j + 1], full) if j >= l else None
                for j in range(GROUP)
            ]
            for l in range(GROUP)
        ]
        rest = [b for b in range(kb, len(blocks)) if b > kb or kr + GROUP < 8]
        cols = {
            b: [jnp.broadcast_to(blocks[b][:, k + j : k + j + 1], full) for j in range(GROUP)]
            for b in rest
        }
        for j in range(GROUP):
            scale = 1.0 / elem[j][j]
            root = lax.rsqrt(elem[j][j])
            done[kb] = jnp.where(sub8 == kr + j, rows[j] * root, done[kb])
            ratio = [
                elem[j][l] * scale if l > j else None for l in range(GROUP)
            ]
            for l in range(j + 1, GROUP):
                rows[l] = rows[l] - ratio[l] * rows[j]
                for m in range(l, GROUP):
                    elem[l][m] = elem[l][m] - ratio[l] * elem[j][m]
            for b in rest:
                mult = cols[b][j] * scale
                if b == kb:
                    mult = jnp.where(sub8 >= kr + GROUP, mult, 0.0)
                blocks[b] = blocks[b] - mult * rows[j]
                for l in range(j + 1, GROUP):
                    cols[b][l] = cols[b][l] - cols[b][j] * ratio[l]
    lower = jnp.concatenate(done, axis=0)
    return dot(
        lower, jnp.concatenate([zeros, wt, zeros, zeros], axis=0), NN, lax.Precision.HIGHEST
    )


def face_penalty(nb, my_slot, slots, links, bases, fractions, speeds, faces, pens, penalty):
    bx = 16
    cy = pens.shape[0]
    mine = lax.fori_loop(
        0, nb, lambda b, acc: jnp.where(slots[b] == my_slot, b, acc), jnp.int32(0)
    )
    upstream = faces[slots[links[0, mine]]]
    downstream = faces[slots[links[1, mine]]]
    own = faces[my_slot]
    lane = lax.broadcasted_iota(jnp.int32, (1, 128), 1)
    node = jnp.zeros((1, 128), jnp.int32)
    frac = jnp.zeros((1, 128), F32)
    for s in range(2):
        for x in range(bx):
            here = (lane // 64 == s) & (lane % bx == x)
            node = jnp.where(here, bases[mine, s, x], node)
            frac = jnp.where(here, fractions[mine, s, x], frac)
    square_row = lax.broadcasted_iota(jnp.int32, (128, 128), 0)
    square_lane = lax.broadcasted_iota(jnp.int32, (128, 128), 1)
    given = square_row % bx
    after = jnp.where(node == bx - 1, 0, node + 1)
    weights = jnp.where(given == node, 1.0 - frac, 0.0) + jnp.where(given == after, frac, 0.0)
    weights = jnp.where(square_row // bx == square_lane // bx, weights, 0.0)
    wide = lax.broadcasted_iota(jnp.int32, (cy, 128), 1)
    donors = pltpu.roll(jnp.where(wide < 64, downstream, upstream), 64, 1)
    inflow = dot(donors, weights, NN, lax.Precision.HIGHEST)
    factor = jnp.where(wide < 64, -2.0 * (speeds[0] + DIFFUSIVITY), -2.0 * DIFFUSIVITY)
    pen = factor * (own - inflow)
    pens[...] = pen
    penalty[...] = jnp.transpose(pen)


def section_rows(v, speed, cells, halo, rates, pens, made):
    nvar, bx, cy, bz = cells.shape
    lane = lax.broadcasted_iota(jnp.int32, (cy, 128), 1)
    row = lax.broadcasted_iota(jnp.int32, (cy, bz), 0)
    factor = (HEAT_RELEASE, -1.0, -OXIDIZER_RATIO, 1.0 + OXIDIZER_RATIO)[v]

    @pl.loop(0, bx, unroll=2)
    def _(x):
        f = cells[v, x]
        around = cells[v, (x + 1) % bx] + cells[v, (x + bx - 1) % bx]
        ahead_y = jnp.where(row == cy - 1, halo[0, v, pl.ds(x, 1), :], pltpu.roll(f, cy - 1, 0))
        behind_y = jnp.where(row == 0, halo[1, v, pl.ds(x, 1), :], pltpu.roll(f, 1, 0))
        ahead = pltpu.roll(f, bz - 1, 1)
        behind = pltpu.roll(f, 1, 1)
        slope = (ahead - behind) * 0.5
        around = (around + ahead_y + behind_y) - 4.0 * f
        curve = (ahead - 2.0 * f) + behind
        base = DIFFUSIVITY * around + factor * rates[x]
        along = DIFFUSIVITY * curve - speed * slope
        made[v, x] = f + TIME_STEP * (base + along)
        at = v * bx + x
        pen = pens[...]
        low = jnp.sum(jnp.where(lane == at, pen, 0.0), axis=1, keepdims=True)
        high = jnp.sum(jnp.where(lane == at + 64, pen, 0.0), axis=1, keepdims=True)
        f0 = f[:, 0:128]
        f1 = pltpu.roll(f0, 127, 1)
        f2 = pltpu.roll(f0, 126, 1)
        edge = DIFFUSIVITY * ((f0 - 2.0 * f1) + f2) - speed * (f1 - f0) + low
        made[v, x, :, 0:128] = f0 + TIME_STEP * (
            base[:, 0:128] + jnp.where(lane == 0, edge, along[:, 0:128])
        )
        f0 = f[:, bz - 128 : bz]
        f1 = pltpu.roll(f0, 1, 1)
        f2 = pltpu.roll(f0, 2, 1)
        edge = DIFFUSIVITY * ((f0 - 2.0 * f1) + f2) - speed * (f0 - f1) + high
        made[v, x, :, bz - 128 : bz] = f0 + TIME_STEP * (
            base[:, bz - 128 : bz] + jnp.where(lane == 127, edge, along[:, bz - 128 : bz])
        )


def finish_kernel(
    made, penalty, vt, snap, out, penalty_out, vt_out, core_out, held, load_sem, store_sem
):
    parts = [(v, pl.ds(x, 8)) for v in range(held.shape[0]) for x in range(0, held.shape[1], 8)]
    loads = [
        pltpu.make_async_copy(made.at[v, x], held.at[v, x], load_sem.at[i])
        for i, (v, x) in enumerate(parts)
    ]
    stores = [
        pltpu.make_async_copy(held.at[v, x], out.at[v, x], store_sem.at[i])
        for i, (v, x) in enumerate(parts)
    ]
    for load in loads:
        load.start()
    for load, store in zip(loads, stores):
        load.wait()
        store.start()
    mode = vt.shape[1]
    penalty_out[...] = penalty[...]
    vt_out[...] = vt[...]
    core_out[...] = join3(dot(split3(vt[...]), snap[...], NT)) * (1.0 / math.sqrt(mode))
    for store in stores:
        store.wait()


def basis_kernel(
    sizes,
    slots,
    links,
    bases,
    fractions,
    speeds,
    fields,
    start,
    vt_out,
    snap,
    made_out,
    penalty,
    cells,
    made,
    picked,
    rates,
    pens,
    faces_in,
    halo,
    edges,
    face_src,
    send_buf,
    recv_buf,
    piece_buf,
    cross_buf,
    whole_buf,
    load_sem,
    rs_send,
    rs_recv,
    ag_send,
    ag_recv,
    cr_send,
    cr_recv,
    face_send,
    face_recv,
    halo_send,
    halo_recv,
    store_sem,
):
    nb, ns, total = sizes
    blk = lax.axis_index("blk")
    sub = lax.axis_index("sub")
    me = blk * ns + sub
    devices = nb * ns
    groups = devices // PIECES
    team, place = me // PIECES, me % PIECES
    nvar, bx, cy, bz = cells.shape
    mode = snap.shape[1]

    def where_is(index):
        return (index // ns, index % ns)

    loads = [
        pltpu.make_async_copy(fields.at[v], cells.at[v], load_sem.at[v]) for v in range(nvar)
    ]
    for load in loads:
        load.start()

    barrier = pltpu.get_barrier_semaphore()

    @pl.loop(1, devices)
    def _(k):
        pl.semaphore_signal(
            barrier, inc=1, device_id=where_is((me + k) % devices), device_id_type=MESH
        )

    vt = start[...]
    pick = (
        lax.broadcasted_iota(jnp.int32, (256, 128), 0)
        == 2 * lax.broadcasted_iota(jnp.int32, (256, 128), 1)
    ).astype(F32).astype(BF16)
    pick_rows = (
        lax.broadcasted_iota(jnp.int32, (128, 256), 1)
        == 2 * lax.broadcasted_iota(jnp.int32, (128, 256), 0)
    ).astype(F32).astype(BF16)
    for v in range(nvar):
        loads[v].wait()
        for xe in range(bx // 2):
            at = (v * (bx // 2) + xe) * cy
            picked[at : at + cy, :] = (cells[v, 2 * xe] - LEVELS[v]).astype(BF16)
    for h in range(2):
        for j in range(mode // 128):
            part = dot(
                picked[256 * h : 256 * h + 256, 256 * j : 256 * j + 256], pick, NN
            ).astype(BF16)
            snap[128 * h : 128 * h + 128, 128 * j : 128 * j + 128] = dot(
                pick_rows, part, NN
            ).astype(BF16)

    def send_faces():
        lane = lax.broadcasted_iota(jnp.int32, (cy, 128), 1)
        face = jnp.zeros((cy, 128), F32)
        for v in range(nvar):
            for x in range(bx):
                low = jnp.broadcast_to(cells[v, x, :, 0:128][:, 0:1], (cy, 128))
                high = jnp.broadcast_to(
                    cells[v, x, :, bz - 128 : bz][:, 127:128], (cy, 128)
                )
                face = jnp.where(lane == v * bx + x, low, face)
                face = jnp.where(lane == 64 + v * bx + x, high, face)
        face_src[...] = face
        faces_in[pl.ds(blk, 1)] = face[None]

        @pl.loop(1, nb)
        def _(k):
            pltpu.make_async_remote_copy(
                src_ref=face_src,
                dst_ref=faces_in.at[blk],
                send_sem=face_send,
                recv_sem=face_recv,
                device_id=((blk + k) % nb, sub),
                device_id_type=MESH,
            ).start()

        for v in range(nvar):
            edges[0, v] = cells[v, :, 0, :]
            edges[1, v] = cells[v, :, cy - 1, :]

    def send_edges(v):
        for side, step in ((0, ns - 1), (1, 1)):
            pltpu.make_async_remote_copy(
                src_ref=edges.at[side, v],
                dst_ref=halo.at[side, v],
                send_sem=halo_send.at[side, v],
                recv_sem=halo_recv.at[side, v],
                device_id=(blk, (sub + step) % ns),
                device_id_type=MESH,
            ).start()

    def build_rates():
        @pl.loop(0, bx)
        def _(x):
            rates[x] = PREFACTOR * cells[1, x] * cells[2, x] * jnp.exp(-ACTIVATION / cells[0, x])

    def build_penalty():
        landed = faces_in.at[pl.ds(0, nb - 1)]
        pltpu.make_async_copy(landed, landed, face_recv).wait()
        face_penalty(nb, blk, slots, links, bases, fractions, speeds, faces_in, pens, penalty)

    def build_section(v):
        for side in range(2):
            landed = halo.at[side, v]
            pltpu.make_async_copy(landed, landed, halo_recv.at[side, v]).wait()
        section_rows(v, speeds[0], cells, halo, rates, pens, made)
        pltpu.make_async_copy(made.at[v], made_out.at[v], store_sem.at[v]).start()

    def fill(slot):
        if slot == 0:
            send_faces()
        if slot < 4:
            send_edges(slot)
        if slot == 1:
            build_rates()
        if slot == 2:
            build_penalty()
        if 3 <= slot < 3 + nvar:
            build_section(slot - 3)

    inv_total = 1.0 / total
    for it in range(ITERS):
        partial = join3(dot(split3(vt), snap[...], NT)) * inv_total
        partial = join3(dot(split3(partial), snap[...], NN))
        for g in range(8):
            for j in range(4):
                send_buf[it, g * 4 + j] = partial[4 * g : 4 * g + 4, 128 * j : 128 * j + 128]
        if it == 0:
            pl.semaphore_wait(barrier, devices - 1)

        @pl.loop(1, PIECES)
        def _(k):
            other = (place + k) % PIECES
            pltpu.make_async_remote_copy(
                src_ref=send_buf.at[it, other],
                dst_ref=recv_buf.at[it, place],
                send_sem=rs_send.at[it],
                recv_sem=rs_recv.at[it],
                device_id=where_is(team * PIECES + other),
                device_id_type=MESH,
            ).start()

        recv_buf[it, pl.ds(place, 1)] = send_buf[it, pl.ds(place, 1)]

        fill(2 * it)
        landed = recv_buf.at[it, pl.ds(0, PIECES - 1)]
        pltpu.make_async_copy(landed, landed, rs_recv.at[it]).wait()
        piece = jnp.sum(recv_buf[it], axis=0)
        if groups > 1:
            piece_buf[it, 0] = piece
            cross_buf[it, pl.ds(team, 1)] = piece[None]

            @pl.loop(1, groups)
            def _(k):
                pltpu.make_async_remote_copy(
                    src_ref=piece_buf.at[it, 0],
                    dst_ref=cross_buf.at[it, team],
                    send_sem=cr_send.at[it],
                    recv_sem=cr_recv.at[it],
                    device_id=where_is(((team + k) % groups) * PIECES + place),
                    device_id_type=MESH,
                ).start()

            crossed = cross_buf.at[it, pl.ds(0, groups - 1)]
            pltpu.make_async_copy(crossed, crossed, cr_recv.at[it]).wait()
            piece = jnp.sum(cross_buf[it], axis=0)
        piece_buf[it, 1] = piece
        whole_buf[it, pl.ds(place, 1)] = piece[None]

        @pl.loop(1, PIECES)
        def _(k):
            pltpu.make_async_remote_copy(
                src_ref=piece_buf.at[it, 1],
                dst_ref=whole_buf.at[it, place],
                send_sem=ag_send.at[it],
                recv_sem=ag_recv.at[it],
                device_id=where_is(team * PIECES + (place + k) % PIECES),
                device_id_type=MESH,
            ).start()

        fill(2 * it + 1)
        gathered = whole_buf.at[it, pl.ds(0, PIECES - 1)]
        pltpu.make_async_copy(gathered, gathered, ag_recv.at[it]).wait()
        wt = jnp.concatenate(
            [
                jnp.concatenate([whole_buf[it, g * 4 + j] for j in range(4)], axis=1)
                for g in range(8)
            ],
            axis=0,
        )
        vt = factor_apply(wt)

    vt_out[...] = vt

    for it in range(ITERS):
        landed = recv_buf.at[it, pl.ds(0, PIECES - 1)]
        pltpu.make_async_copy(landed, landed, rs_send.at[it]).wait()
        pltpu.make_async_copy(landed, landed, ag_send.at[it]).wait()
        if groups > 1:
            crossed = cross_buf.at[it, pl.ds(0, groups - 1)]
            pltpu.make_async_copy(crossed, crossed, cr_send.at[it]).wait()
        for side in range(2):
            pltpu.make_async_copy(
                edges.at[side, it], edges.at[side, it], halo_send.at[side, it]
            ).wait()
    for v in range(nvar):
        pltpu.make_async_copy(made.at[v], made_out.at[v], store_sem.at[v]).wait()
    gathered = faces_in.at[pl.ds(0, nb - 1)]
    pltpu.make_async_copy(gathered, gathered, face_send).wait()


def per_device(nb, ns, fields, block_speed, neighbours, block_slot, table_base, table_weight, start_basis):
    local = fields[0]
    nvar, bx, cy, bz = local.shape
    mode, rank = start_basis.shape
    rows = nvar * (bx // 2) * (cy // 2)
    groups = nb * ns // PIECES
    vmem = pl.BlockSpec(memory_space=pltpu.VMEM)
    smem = pl.BlockSpec(memory_space=pltpu.SMEM)
    dma = pltpu.SemaphoreType.DMA
    vt, snap, made, penalty = pl.pallas_call(
        functools.partial(basis_kernel, (nb, ns, rows * nb * ns)),
        out_shape=(
            jax.ShapeDtypeStruct((rank, mode), F32),
            jax.ShapeDtypeStruct((rows, mode), BF16),
            jax.ShapeDtypeStruct((nvar, bx, cy, bz), F32),
            jax.ShapeDtypeStruct((128, cy), F32),
        ),
        in_specs=[smem] * 5 + [pl.BlockSpec(memory_space=pltpu.HBM), vmem],
        out_specs=(vmem, vmem, pl.BlockSpec(memory_space=pltpu.HBM), vmem),
        scratch_shapes=[
            pltpu.VMEM((nvar, bx, cy, bz), F32),
            pltpu.VMEM((nvar, bx, cy, bz), F32),
            pltpu.VMEM((2 * rows, bz), BF16),
            pltpu.VMEM((bx, cy, bz), F32),
            pltpu.VMEM((cy, 128), F32),
            pltpu.VMEM((nb, cy, 128), F32),
            pltpu.VMEM((2, nvar, bx, bz), F32),
            pltpu.VMEM((2, nvar, bx, bz), F32),
            pltpu.VMEM((cy, 128), F32),
            pltpu.VMEM((ITERS, PIECES, 4, 128), F32),
            pltpu.VMEM((ITERS, PIECES, 4, 128), F32),
            pltpu.VMEM((ITERS, 2, 4, 128), F32),
            pltpu.VMEM((ITERS, max(groups, 2), 4, 128), F32),
            pltpu.VMEM((ITERS, PIECES, 4, 128), F32),
            dma((nvar,)),
            dma((ITERS,)),
            dma((ITERS,)),
            dma((ITERS,)),
            dma((ITERS,)),
            dma((ITERS,)),
            dma((ITERS,)),
            dma,
            dma,
            dma((2, ITERS)),
            dma((2, ITERS)),
            dma((nvar,)),
        ],
        compiler_params=pltpu.CompilerParams(
            collective_id=0, has_side_effects=True, vmem_limit_bytes=60 * 1024 * 1024
        ),
        name="basis",
    )(block_slot, neighbours.T, table_base, table_weight, block_speed, local, start_basis.T)
    section, penalty, vt, core = pl.pallas_call(
        finish_kernel,
        out_shape=(
            jax.ShapeDtypeStruct((nvar, bx, cy, bz), F32),
            jax.ShapeDtypeStruct((128, cy), F32),
            jax.ShapeDtypeStruct((rank, mode), F32),
            jax.ShapeDtypeStruct((rank, rows), F32),
        ),
        in_specs=[pl.BlockSpec(memory_space=pl.ANY), vmem, vmem, vmem],
        out_specs=(pl.BlockSpec(memory_space=pltpu.HBM), vmem, vmem, vmem),
        scratch_shapes=[
            pltpu.VMEM((nvar, bx, cy, bz), F32),
            dma((2 * nvar,)),
            dma((2 * nvar,)),
        ],
        compiler_params=pltpu.CompilerParams(vmem_limit_bytes=60 * 1024 * 1024),
        name="finish",
    )(made, penalty, vt, snap)
    return (
        section[None],
        penalty.reshape(1, 2, nvar, bx, cy),
        vt.T,
        core,
    )


def solution(mesh):
    in_specs = (P("blk", None, None, "sub", None), P("blk"), P(), P(), P(), P(), P())
    out_specs = (
        P("blk", None, None, "sub", None),
        P("blk", None, None, None, "sub"),
        P(),
        P(None, ("blk", "sub")),
    )
    body = functools.partial(per_device, mesh.shape["blk"], mesh.shape["sub"])
    return jax.shard_map(
        body, mesh=mesh, in_specs=in_specs, out_specs=out_specs, check_vma=False
    )
```
